256 devices in a mesh: pipe: 32 (over z_lo, x, core), tensor: 8 (over y, z_hi).
Axes of the slice: x: 4, y: 4, z: 8 (z_hi: 2, z_lo: 4; z = z_hi * 4 + z_lo), core: 2. Of those that a mesh axis runs over, the one named last changes fastest.
Arguments:
- down_prev: bfloat16 [32, 256, 4096], P('pipe', 'tensor'), may hold values from -6 to 6
- up_prev: bfloat16 [32, 256, 4096], P('pipe', 'tensor'), may hold values from -6 to 6
- down_stash: bfloat16 [32, 256, 4096], P('pipe', 'tensor'), may hold values from -6 to 6
- up_stash: bfloat16 [32, 256, 4096], P('pipe', 'tensor'), may hold values from -6 to 6
- down_cot: bfloat16 [32, 256, 4096], P('pipe', 'tensor'), may hold values from -0.75 to 0.75
- up_cot: bfloat16 [32, 256, 4096], P('pipe', 'tensor'), may hold values from -0.75 to 0.75
- boundary: bfloat16 [4, 256, 4096], P(None, 'tensor'), may hold values from -3 to 3
- segment_ids: int32 [4, 32, 256], P(None, 'pipe'), may hold values from 0 to 31, never falling along the last dimension, each value on 1 to 128 neighbouring positions
- value_weight: bfloat16 [32, 2, 4096, 1024], P('pipe', None, None, 'tensor'), as said below
- output_weight: bfloat16 [32, 2, 1024, 4096], P('pipe', None, 'tensor'), as said below
Outputs:
- down_out: bfloat16 [32, 256, 4096], P('pipe', 'tensor')
- up_out: bfloat16 [32, 256, 4096], P('pipe', 'tensor')
- down_back: bfloat16 [32, 256, 4096], P('pipe', 'tensor')
- up_back: bfloat16 [32, 256, 4096], P('pipe', 'tensor')
- value_grad: float32 [32, 4096, 1024], P('pipe', None, 'tensor')
- output_grad: float32 [32, 1024, 4096], P('pipe', 'tensor')
The draws below stay inside these ranges and needn't reach their ends.
Inputs may be any that keep to these rules, and one draw needn't show every extreme that they name: `segment_ids`: ids never fall along a micro-batch's tokens. `value_weight`: entry [r, 1] equals entry [31 - r, 0]: both copies of a section are equal. `output_weight`: entry [r, 1] equals entry [31 - r, 0]: both copies of a section are equal.
All inputs are finite; a program needn't handle non-finite values.
Results may differ from the reference program's by a relative error of at most 0.012.
Values may be sent and summed in bfloat16 or wider, within the bound.
No kernel may reach another device: no remote copies, remote signals or barrier semaphores. Data moves between devices by JAX's collectives and lax.ppermute only.
A program may use at most 128 MiB of HBM per device.

```python
import math
import jax
import jax.numpy as jnp
import numpy as np
from jax import lax

D = 4096
HEAD = 128
HEADS = 8
VALUE_WIDTH = 1024
TOK = 256
N_PIPE = 32


def mirrored(section_draw):
    return jnp.stack([section_draw, jnp.flip(section_draw, 0)], axis=1).astype(jnp.bfloat16)


def draw_value_weight(key, part):
    key = jax.random.fold_in(key, 11)
    dims_all = (N_PIPE, D, VALUE_WIDTH)
    section_draw = jax.random.normal(key, dims_all, jnp.float32)
    return mirrored(section_draw * D ** (-0.5))


def draw_output_weight(key, part):
    key = jax.random.fold_in(key, 23)
    dims_all = (N_PIPE, VALUE_WIDTH, D)
    section_draw = jax.random.normal(key, dims_all, jnp.float32)
    return mirrored(section_draw * VALUE_WIDTH ** (-0.5))


def steps_of(key, extent, pieces, least, top_value):
    loudness, own = 1.0, jax.random.fold_in(key, 6)
    for position, shards_of in pieces:
        draws = jnp.exp(jax.random.uniform(jax.random.fold_in(own, position), (shards_of,), jnp.float32, least / len(pieces), top_value / len(pieces)))
        loudness = loudness * jnp.repeat(draws, extent[position] // shards_of).reshape([-1 if axis == position else 1 for axis in range(len(extent))])
    return loudness


def profile(count, total, limit, lean):
    loads = [(1 << 20) // math.isqrt(grade ** lean) + 1 for grade in range(2, count + 1)]
    surplus, given = total - limit - (count - 1), [1] * (count - 1)
    while surplus > 0:
        candidates = [i for i in range(count - 1) if given[i] < limit]
        pool, left = sum([loads[i] for i in candidates]), surplus
        for i in candidates:
            more = min(limit - given[i], max(1, left * loads[i] // pool), surplus)
            given[i] = given[i] + more
            surplus = surplus - more
    return np.array([limit] + given)


def ragged(own_key, number_of, total, limit, skew):
    if number_of == 2:
        one = jax.random.randint(own_key, (), max(1, total - limit), min(limit, total - 1) + 1)
        return jnp.stack([one, total - one])
    lengths = jnp.asarray(profile(number_of, total, limit, skew), jnp.int32)
    couples = (number_of - 1) // 2
    donor, taker = lengths[1:1 + 2 * couples:2], lengths[2:2 + 2 * couples:2]
    room = jnp.minimum(donor - 1, limit - taker)
    passed = jax.random.randint(jax.random.fold_in(own_key, 1), (couples,), 0, 1 << 20) % (room + 1)
    lengths = lengths.at[1:1 + 2 * couples:2].set(donor - passed).at[2:2 + 2 * couples:2].set(taker + passed)
    return lengths[jax.random.permutation(jax.random.fold_in(own_key, 2), number_of)]


def normal_values(key, shape, deviation, limit, pieces=(), held_as=jnp.bfloat16):
    level = steps_of(key, shape, pieces, -0.22, 0.18) if pieces else 1.0
    drawn = jax.random.normal(key, shape, jnp.float32) * deviation * level
    return jnp.minimum(jnp.maximum(drawn, -limit), limit).astype(held_as)


def setup_inputs(seed: int = 0) -> dict:
    key_of = jax.random.split(jax.random.key(seed), 11)
    return {
        "down_prev": normal_values(key_of[0], (N_PIPE, TOK, D), 1.0, 6.0, ((0, 32), (1, 8))),
        "up_prev": normal_values(key_of[1], (N_PIPE, TOK, D), 1.0, 6.0, ((0, 32), (1, 8))),
        "down_stash": normal_values(key_of[2], (N_PIPE, TOK, D), 1.0, 6.0, ((0, 32), (1, 8))),
        "up_stash": normal_values(key_of[3], (N_PIPE, TOK, D), 1.0, 6.0, ((0, 32), (1, 8))),
        "down_cot": normal_values(key_of[4], (N_PIPE, TOK, D), 0.125, 0.75, ((0, 32), (1, 8))),
        "up_cot": normal_values(key_of[5], (N_PIPE, TOK, D), 0.125, 0.75, ((0, 32), (1, 8))),
        "boundary": normal_values(key_of[6], (4, TOK, D), 0.5, 3.0, ((1, 8),)),
        "segment_ids": jax.vmap(lambda own: jnp.searchsorted(jnp.cumsum(ragged(own, TOK // 8, TOK, TOK // 2, 1)), jnp.arange(TOK), side="right"))(jax.random.split(key_of[7], 4 * N_PIPE)).reshape((4, N_PIPE, TOK)).astype(jnp.int32),
        "value_weight": draw_value_weight(jax.random.fold_in(key_of[10], 71), 0),
        "output_weight": draw_output_weight(jax.random.fold_in(key_of[10], 71), 0),
    }


eps = 1e-05

def segment_mask(segment_row):
    positions = jnp.arange(segment_row.shape[0], dtype=jnp.int32)
    causal = positions[:, None] >= positions[None, :]
    same_segment = segment_row[:, None] == segment_row[None, :]
    allowed = jnp.logical_and(causal, same_segment)
    return (allowed.astype(jnp.bfloat16), lax.optimization_barrier(jnp.sum(allowed.astype(jnp.float32), axis=1, keepdims=True)))

def normalize(inputs):
    widened = inputs.astype(jnp.float32)
    inverse_rms = lax.rsqrt(lax.optimization_barrier(jnp.mean(widened * widened, axis=-1, keepdims=True)) + eps)
    return (widened * inverse_rms, inverse_rms)

def contract(left_side, right_side, left_dim, right_dim):
    return lax.dot_general(left_side, right_side, (((left_dim,), (right_dim,)), ((), ())), preferred_element_type=jnp.float32)

def head_sum(left_side, right_side):
    tokens = left_side.shape[0]
    width_out = right_side.shape[1]
    left_heads = jnp.transpose(left_side.reshape(tokens, HEADS, HEAD), (1, 0, 2))
    right_heads = right_side.reshape(HEADS, HEAD, width_out)

    def add_head(running, operands):
        partial_term = jnp.dot(operands[0], operands[1], preferred_element_type=jnp.float32)
        rounded = lax.optimization_barrier(partial_term.astype(jnp.bfloat16)).astype(jnp.float32)
        return (running + rounded, None)
    start = jnp.zeros((tokens, width_out), jnp.float32)
    total, unused = lax.scan(add_head, start, (left_heads, right_heads))
    return total

def layer_forward(inputs, segment_row, value_proj, output_proj):
    allowed, counts = segment_mask(segment_row)
    normed = normalize(inputs)[0].astype(jnp.bfloat16)
    values = jnp.dot(normed, value_proj, preferred_element_type=jnp.float32).astype(jnp.bfloat16)
    mixed_values = (jnp.dot(allowed, values, preferred_element_type=jnp.float32) / counts).astype(jnp.bfloat16)
    summed = head_sum(mixed_values, output_proj)
    return (inputs.astype(jnp.float32) + summed).astype(jnp.bfloat16)

def layer_backward(inputs, upstream, segment_row, value_proj, output_proj):
    allowed, counts = segment_mask(segment_row)
    normed_full, inverse_rms = normalize(inputs)
    normed = normed_full.astype(jnp.bfloat16)
    values = jnp.dot(normed, value_proj, preferred_element_type=jnp.float32).astype(jnp.bfloat16)
    mixed_values = (jnp.dot(allowed, values, preferred_element_type=jnp.float32) / counts).astype(jnp.bfloat16)
    output_grad = contract(mixed_values, upstream, 0, 0)
    scaled = (contract(upstream, output_proj, 1, 1) / counts).astype(jnp.bfloat16)
    value_act = contract(allowed, scaled, 0, 0).astype(jnp.bfloat16)
    value_grad = contract(normed, value_act, 0, 0)
    normed_grad = head_sum(value_act, jnp.transpose(value_proj))
    project = lax.optimization_barrier(jnp.mean(normed_grad * normed_full, axis=-1, keepdims=True))
    input_grad = upstream.astype(jnp.float32) + inverse_rms * (normed_grad - normed_full * project)
    return (input_grad.astype(jnp.bfloat16), value_grad, output_grad)

def reference(down_prev, up_prev, down_stash, up_stash, down_cot, up_cot, boundary, segment_ids, value_weight, output_weight):
    down_input = jnp.concatenate([boundary[0:1], down_prev[:-1]], axis=0)
    up_input = jnp.concatenate([up_prev[1:], boundary[1:2]], axis=0)
    down_upstream = jnp.concatenate([down_cot[1:], boundary[2:3]], axis=0)
    up_upstream = jnp.concatenate([boundary[3:4], up_cot[:-1]], axis=0)
    segment_ranks = jnp.transpose(segment_ids, (1, 0, 2))

    def rank_step(operands):
        down_x, up_x, down_kept, up_kept, down_grad, up_grad, segment_rows, value_pair, output_pair = operands
        down_result = layer_forward(down_x, segment_rows[0], value_pair[0], output_pair[0])
        up_result = layer_forward(up_x, segment_rows[1], value_pair[1], output_pair[1])
        down_input_grad, down_value, down_output = layer_backward(down_kept, down_grad, segment_rows[2], value_pair[0], output_pair[0])
        up_input_grad, up_value, up_output = layer_backward(up_kept, up_grad, segment_rows[3], value_pair[1], output_pair[1])
        return (down_result, up_result, down_input_grad, up_input_grad, down_value.astype(jnp.bfloat16), down_output.astype(jnp.bfloat16), up_value.astype(jnp.bfloat16), up_output.astype(jnp.bfloat16))
    results = lax.map(rank_step, (down_input, up_input, down_stash, up_stash, down_upstream, up_upstream, segment_ranks, value_weight, output_weight))
    own_value = lax.optimization_barrier(results[4]).astype(jnp.float32)
    own_output = lax.optimization_barrier(results[5]).astype(jnp.float32)
    mirror_value = lax.optimization_barrier(results[6][::-1]).astype(jnp.float32)
    mirror_output = lax.optimization_barrier(results[7][::-1]).astype(jnp.float32)
    return (results[0], results[1], results[2], results[3], own_value + mirror_value, own_output + mirror_output)
```

```python
import jax
import jax.numpy as jnp
from jax import lax
from jax.sharding import PartitionSpec as P

eps = 1e-05

RANKS = 32
LANES = 8
RING = 4


def spot(rank, row, half):
    return (rank % RANKS) * LANES + (row % RING) * 2 + half % 2


def moved(shard, rank_to, row_by=0, half_by=0):
    pairs = [
        (spot(r, y, z), spot(rank_to(r), y + row_by, z + half_by))
        for r in range(RANKS)
        for y in range(RING)
        for z in range(2)
    ]
    return lax.ppermute(shard, ("pipe", "tensor"), pairs)


def stay(r):
    return r


def up_one(r):
    return r + 1


def down_one(r):
    return r - 1


def mirror(r):
    return RANKS - 1 - r


def mirror_next(r):
    return RANKS - 2 - r


def normalize(inputs):
    widened = inputs.astype(jnp.float32)
    inverse_rms = lax.rsqrt(jnp.mean(widened * widened, axis=-1, keepdims=True) + eps)
    return (widened * inverse_rms, inverse_rms)


def contract(left_side, right_side, left_dim, right_dim):
    return lax.dot_general(
        left_side,
        right_side,
        (((left_dim,), (right_dim,)), ((), ())),
        preferred_element_type=jnp.float32,
    )


def token_order():
    lane = lax.axis_index("tensor")
    row, half = lane // 2, lane % 2
    other = 1 - half
    left, right, far = (row + 3) % 4, (row + 1) % 4, (row + 2) % 4
    lanes = jnp.stack(
        [
            row * 2 + half,
            row * 2 + other,
            left * 2 + half,
            left * 2 + other,
            right * 2 + half,
            right * 2 + other,
            far * 2 + half,
            far * 2 + other,
        ]
    )
    return (lanes[:, None] * 32 + jnp.arange(32, dtype=lanes.dtype)[None, :]).reshape(-1)


def segment_mask(segment_row, order):
    segments = segment_row[order]
    causal = order[:, None] >= order[None, :]
    same_segment = segments[:, None] == segments[None, :]
    allowed = jnp.logical_and(causal, same_segment)
    return (
        allowed.astype(jnp.bfloat16),
        jnp.sum(allowed.astype(jnp.float32), axis=1, keepdims=True),
    )


def gather(own, other):
    pair = jnp.concatenate([own, other], axis=0)
    left = moved(pair, stay, 1)
    right = moved(pair, stay, -1)
    far_own = moved(left[:32], stay, 1)
    far_other = moved(right[32:], stay, -1)
    return jnp.concatenate([pair, left, right, far_own, far_other], axis=0)


def scatter(act, weight, weight_dim):
    def rows(lo, hi):
        return contract(act[lo:hi], weight, 1, weight_dim)

    far = rows(192, 256).astype(jnp.bfloat16)
    add_left = moved(far[:32], stay, -1).astype(jnp.float32)
    add_right = moved(far[32:], stay, 1).astype(jnp.float32)
    none = jnp.zeros_like(add_left)
    left = rows(64, 128) + jnp.concatenate([add_left, none], axis=0)
    right = rows(128, 192) + jnp.concatenate([none, add_right], axis=0)
    from_right = moved(left.astype(jnp.bfloat16), stay, -1).astype(jnp.float32)
    from_left = moved(right.astype(jnp.bfloat16), stay, 1).astype(jnp.float32)
    return rows(0, 64) + from_right + from_left


def values_of(normed, allowed, counts, value_proj):
    values = jnp.dot(normed, value_proj, preferred_element_type=jnp.float32).astype(jnp.bfloat16)
    return (jnp.dot(allowed, values, preferred_element_type=jnp.float32) / counts).astype(
        jnp.bfloat16
    )


def local(
    down_prev,
    up_prev,
    down_stash,
    up_stash,
    down_cot,
    up_cot,
    boundary,
    segment_ids,
    value_weight,
    output_weight,
):
    rank = lax.axis_index("pipe")
    is_first = rank == 0
    is_last = rank == RANKS - 1
    order = token_order()

    send_down = jnp.where(is_last, boundary[0], down_prev[0])
    send_up = jnp.where(is_first, boundary[1], up_prev[0])
    send_down_cot = jnp.where(is_first, boundary[2], down_cot[0])
    send_up_cot = jnp.where(is_last, boundary[3], up_cot[0])

    value_proj, output_proj = value_weight[0, 0], output_weight[0, 0]

    down_normed, down_inverse = normalize(down_stash[0])
    up_normed, up_inverse = normalize(up_stash[0])
    down_normed16 = down_normed.astype(jnp.bfloat16)
    up_normed16 = up_normed.astype(jnp.bfloat16)

    down_grad = moved(send_down_cot, down_one)
    up_grad = moved(send_up_cot, up_one)
    mirrored_ids = moved(segment_ids[3, 0], mirror)

    kept = (
        gather(down_normed16, moved(down_normed16, stay, 0, 1)),
        gather(moved(up_normed16, mirror), moved(up_normed16, mirror, 0, 1)),
    )
    cots = (
        gather(down_grad, moved(send_down_cot, down_one, 0, 1)),
        gather(moved(send_up_cot, mirror_next), moved(send_up_cot, mirror_next, 0, 1)),
    )
    masks = (segment_mask(segment_ids[2, 0], order), segment_mask(mirrored_ids, order))
    mixed = []
    acts = []
    sums = []
    for job in range(2):
        allowed, counts = masks[job]
        mixed.append(values_of(kept[job], allowed, counts, value_proj))
        scaled = (contract(cots[job], output_proj, 1, 1) / counts).astype(jnp.bfloat16)
        acts.append(contract(allowed, scaled, 0, 0).astype(jnp.bfloat16))
        sums.append(scatter(acts[job], value_proj, 1))

    value_grad = contract(
        jnp.concatenate(kept, axis=0), jnp.concatenate(acts, axis=0), 0, 0
    )
    output_grad = contract(
        jnp.concatenate(mixed, axis=0), jnp.concatenate(cots, axis=0), 0, 0
    )

    down_sum = sums[0][:32] + moved(sums[0][32:].astype(jnp.bfloat16), stay, 0, 1).astype(
        jnp.float32
    )
    up_sums = sums[1].astype(jnp.bfloat16)
    up_sum = moved(up_sums[:32], mirror).astype(jnp.float32) + moved(
        up_sums[32:], mirror, 0, 1
    ).astype(jnp.float32)

    def input_grad(own_grad, own_normed, own_inverse, normed_grad):
        project = jnp.mean(normed_grad * own_normed, axis=-1, keepdims=True)
        out = own_grad.astype(jnp.float32) + own_inverse * (normed_grad - own_normed * project)
        return out.astype(jnp.bfloat16)

    down_back = input_grad(down_grad, down_normed, down_inverse, down_sum)
    up_back = input_grad(up_grad, up_normed, up_inverse, up_sum)

    forward = []
    for send, by, job in ((send_down, up_one, 0), (send_up, down_one, 1)):
        own = moved(send, by)
        other = moved(normalize(send)[0].astype(jnp.bfloat16), by, 0, 1)
        normed = gather(normalize(own)[0].astype(jnp.bfloat16), other)
        allowed, counts = segment_mask(segment_ids[job, 0], order)
        mix = values_of(normed, allowed, counts, value_weight[0, job])
        total = scatter(mix, output_weight[0, job], 0)
        added = total[:32] + moved(total[32:].astype(jnp.bfloat16), stay, 0, 1).astype(
            jnp.float32
        )
        forward.append((own.astype(jnp.float32) + added).astype(jnp.bfloat16))

    return (
        forward[0][None],
        forward[1][None],
        down_back[None],
        up_back[None],
        value_grad[None],
        output_grad[None],
    )


def solution(mesh):
    placed = (
        P("pipe", "tensor", None),
        P("pipe", "tensor", None),
        P("pipe", "tensor", None),
        P("pipe", "tensor", None),
        P("pipe", "tensor", None),
        P("pipe", "tensor", None),
        P(None, "tensor", None),
        P(None, "pipe", None),
        P("pipe", None, None, "tensor"),
        P("pipe", None, "tensor", None),
    )
    return jax.shard_map(
        local,
        mesh=mesh,
        in_specs=placed,
        out_specs=(
            P("pipe", "tensor", None),
            P("pipe", "tensor", None),
            P("pipe", "tensor", None),
            P("pipe", "tensor", None),
            P("pipe", None, "tensor"),
            P("pipe", "tensor", None),
        ),
        check_vma=False,
    )
```

```python
import jax
import jax.numpy as jnp
from jax import lax
from jax.sharding import PartitionSpec as P

eps = 1e-05

RANKS = 32
LANES = 8
RING = 4
ROWS = 32


def spot(rank, row, half):
    return (rank % RANKS) * LANES + (row % RING) * 2 + half % 2


def moved(shard, rank_to, half_by=0):
    pairs = [
        (spot(r, y, z), spot(rank_to(r), y, z + half_by))
        for r in range(RANKS)
        for y in range(RING)
        for z in range(2)
    ]
    return lax.ppermute(shard, ("pipe", "tensor"), pairs)


def stay(r):
    return r


def up_one(r):
    return r + 1


def down_one(r):
    return r - 1


def mirror(r):
    return RANKS - 1 - r


def mirror_next(r):
    return RANKS - 2 - r


def mirror_prev(r):
    return RANKS - r


def turned(blocks):
    return lax.all_to_all(
        blocks,
        "tensor",
        split_axis=0,
        concat_axis=0,
        axis_index_groups=[[0, 2, 4, 6], [1, 3, 5, 7]],
        tiled=True,
    )


def shared(block):
    return turned(jnp.broadcast_to(block[None], (RING,) + block.shape))


def columns_out(rows):
    k, n, d = rows.shape
    return turned(rows.reshape(k, n, RING, d // RING).transpose(2, 0, 1, 3))


def columns_back(blocks):
    back = turned(blocks)
    q, k, n, c = back.shape
    return back.transpose(1, 2, 0, 3).reshape(k, n, q * c)


def normalize(inputs):
    widened = inputs.astype(jnp.float32)
    inverse_rms = lax.rsqrt(jnp.mean(widened * widened, axis=-1, keepdims=True) + eps)
    return (widened * inverse_rms, inverse_rms)


def product(spec, left, right):
    return jnp.einsum(spec, left, right, preferred_element_type=jnp.float32)


def token_order():
    half = lax.axis_index("tensor") % 2
    halves = jnp.stack([half, 1 - half])
    rows = jnp.arange(RING, dtype=jnp.int32)
    within = jnp.arange(ROWS, dtype=jnp.int32)
    lanes = rows[None, :] * 2 + halves[:, None]
    return (lanes[:, :, None] * ROWS + within[None, None, :]).reshape(-1)


def segment_mask(segment_row, order):
    by_half = segment_row.reshape(RING, 2, ROWS).transpose(1, 0, 2)
    half = lax.axis_index("tensor") % 2
    segments = jnp.where(half == 0, by_half, by_half[::-1]).reshape(-1)
    causal = order[:, None] >= order[None, :]
    same_segment = segments[:, None] == segments[None, :]
    allowed = jnp.logical_and(causal, same_segment)
    return (
        allowed.astype(jnp.bfloat16),
        jnp.sum(allowed.astype(jnp.float32), axis=1, keepdims=True),
    )


def summed_over_ring(parts):
    return jnp.sum(turned(parts.astype(jnp.bfloat16)).astype(jnp.float32), axis=0)


def mixed_of(normed, masks, value_cols):
    values = summed_over_ring(product("rd,hdk->hrk", normed, value_cols)).astype(jnp.bfloat16)
    tokens = values.shape[0] // 2
    return jnp.concatenate(
        [
            (
                jnp.dot(
                    allowed,
                    values[job * tokens : (job + 1) * tokens],
                    preferred_element_type=jnp.float32,
                )
                / counts
            ).astype(jnp.bfloat16)
            for job, (allowed, counts) in enumerate(masks)
        ]
    )


def home(sums):
    by_half = sums.reshape(2, 2, RING, ROWS, -1)
    down = by_half[0, 0] + moved(by_half[0, 1].astype(jnp.bfloat16), stay, 1).astype(jnp.float32)
    up16 = by_half[1].astype(jnp.bfloat16)
    up = moved(up16[0], mirror).astype(jnp.float32) + moved(up16[1], mirror, 1).astype(jnp.float32)
    return columns_back(jnp.stack([down, up], axis=1).astype(jnp.bfloat16))


def local(
    down_prev,
    up_prev,
    down_stash,
    up_stash,
    down_cot,
    up_cot,
    boundary,
    segment_ids,
    value_weight,
    output_weight,
):
    rank = lax.axis_index("pipe")
    is_first = rank == 0
    is_last = rank == RANKS - 1
    order = token_order()

    send_down = jnp.where(is_last, boundary[0], down_prev[0])
    send_up = jnp.where(is_first, boundary[1], up_prev[0])
    send_down_cot = jnp.where(is_first, boundary[2], down_cot[0])
    send_up_cot = jnp.where(is_last, boundary[3], up_cot[0])

    mirrored_ids = moved(segment_ids[:, 0], mirror)
    forward_masks = (
        segment_mask(segment_ids[0, 0], order),
        segment_mask(mirrored_ids[1], order),
    )
    backward_masks = (
        segment_mask(segment_ids[2, 0], order),
        segment_mask(mirrored_ids[3], order),
    )

    cots = columns_out(jnp.stack([send_down_cot, send_up_cot]))
    down_g, up_g = cots[:, 0], cots[:, 1]
    grad_rows = jnp.concatenate(
        [
            moved(down_g, down_one).reshape(-1, down_g.shape[-1]),
            moved(down_g, down_one, 1).reshape(-1, down_g.shape[-1]),
            moved(up_g, mirror_next).reshape(-1, up_g.shape[-1]),
            moved(up_g, mirror_next, 1).reshape(-1, up_g.shape[-1]),
        ]
    )

    head, width = output_weight.shape[2:]
    output_cols = turned(
        output_weight[0, 0].reshape(head, RING, width // RING).transpose(1, 0, 2)
    )
    value_cols = turned(value_weight[0, 0].reshape(RING, width // RING, head))

    sent = columns_out(
        jnp.stack(
            [
                normalize(send_down)[0].astype(jnp.bfloat16),
                normalize(send_up)[0].astype(jnp.bfloat16),
            ]
        )
    )
    down_x, up_x = sent[:, 0], sent[:, 1]
    forward_rows = jnp.concatenate(
        [
            moved(down_x, up_one).reshape(-1, down_x.shape[-1]),
            moved(down_x, up_one, 1).reshape(-1, down_x.shape[-1]),
            moved(up_x, mirror_prev).reshape(-1, up_x.shape[-1]),
            moved(up_x, mirror_prev, 1).reshape(-1, up_x.shape[-1]),
        ]
    )

    down_normed, down_inverse = normalize(down_stash[0])
    up_normed, up_inverse = normalize(up_stash[0])
    kept = columns_out(jnp.stack([down_normed, up_normed]).astype(jnp.bfloat16))
    down_n, up_n = kept[:, 0], kept[:, 1]
    kept_rows = jnp.concatenate(
        [
            down_n.reshape(-1, down_n.shape[-1]),
            moved(down_n, stay, 1).reshape(-1, down_n.shape[-1]),
            moved(up_n, mirror).reshape(-1, up_n.shape[-1]),
            moved(up_n, mirror, 1).reshape(-1, up_n.shape[-1]),
        ]
    )

    from_below = moved(jnp.stack([send_down, send_up_cot]), up_one)
    from_above = moved(jnp.stack([send_up, send_down_cot]), down_one)

    scaled = summed_over_ring(product("rd,hkd->hrk", grad_rows, output_cols))
    tokens = scaled.shape[0] // 2
    acts = shared(
        jnp.concatenate(
            [
                contract_rows(
                    allowed,
                    (scaled[job * tokens : (job + 1) * tokens] / counts).astype(jnp.bfloat16),
                ).astype(jnp.bfloat16)
                for job, (allowed, counts) in enumerate(backward_masks)
            ]
        )
    )
    normed_grads = home(product("hrk,hdk->rd", acts, value_cols)).astype(jnp.float32)

    def input_grad(own_grad, own_normed, own_inverse, normed_grad):
        project = jnp.mean(normed_grad * own_normed, axis=-1, keepdims=True)
        out = own_grad.astype(jnp.float32) + own_inverse * (normed_grad - own_normed * project)
        return out.astype(jnp.bfloat16)

    down_back = input_grad(from_above[1], down_normed, down_inverse, normed_grads[0])
    up_back = input_grad(from_below[1], up_normed, up_inverse, normed_grads[1])

    forward_mixed = shared(mixed_of(forward_rows, forward_masks, value_cols))
    added = home(product("hrk,hkd->rd", forward_mixed, output_cols)).astype(jnp.float32)
    down_out = (from_below[0].astype(jnp.float32) + added[0]).astype(jnp.bfloat16)
    up_out = (from_above[0].astype(jnp.float32) + added[1]).astype(jnp.bfloat16)

    value_grad = turned(product("rd,hrk->hdk", kept_rows, acts).astype(jnp.bfloat16))
    kept_mixed = shared(mixed_of(kept_rows, backward_masks, value_cols))
    output_grad = turned(product("hrk,rd->hkd", kept_mixed, grad_rows).astype(jnp.bfloat16))

    return (
        down_out[None],
        up_out[None],
        down_back[None],
        up_back[None],
        value_grad.reshape(width, head).astype(jnp.float32)[None],
        output_grad.transpose(1, 0, 2).reshape(head, width).astype(jnp.float32)[None],
    )


def contract_rows(left, right):
    return lax.dot_general(
        left, right, (((0,), (0,)), ((), ())), preferred_element_type=jnp.float32
    )


def solution(mesh):
    placed = (
        P("pipe", "tensor", None),
        P("pipe", "tensor", None),
        P("pipe", "tensor", None),
        P("pipe", "tensor", None),
        P("pipe", "tensor", None),
        P("pipe", "tensor", None),
        P(None, "tensor", None),
        P(None, "pipe", None),
        P("pipe", None, None, "tensor"),
        P("pipe", None, "tensor", None),
    )
    return jax.shard_map(
        local,
        mesh=mesh,
        in_specs=placed,
        out_specs=(
            P("pipe", "tensor", None),
            P("pipe", "tensor", None),
            P("pipe", "tensor", None),
            P("pipe", "tensor", None),
            P("pipe", None, "tensor"),
            P("pipe", "tensor", None),
        ),
        check_vma=False,
    )
```

```python
import jax
import jax.numpy as jnp
from jax import lax
from jax.sharding import PartitionSpec as P

eps = 1e-05

RANKS = 32
LANES = 8
RING = 4
ROWS = 32


def spot(rank, row, half):
    return (rank % RANKS) * LANES + (row % RING) * 2 + half % 2


def moved(shard, rank_to, half_by=0):
    pairs = [
        (spot(r, y, z), spot(rank_to(r), y, z + half_by))
        for r in range(RANKS)
        for y in range(RING)
        for z in range(2)
    ]
    return lax.ppermute(shard, ("pipe", "tensor"), pairs)


def stay(r):
    return r


def up_one(r):
    return r + 1


def down_one(r):
    return r - 1


def mirror(r):
    return RANKS - 1 - r


def mirror_next(r):
    return RANKS - 2 - r


def turned(blocks):
    return lax.all_to_all(
        blocks,
        "tensor",
        split_axis=0,
        concat_axis=0,
        axis_index_groups=[[0, 2, 4, 6], [1, 3, 5, 7]],
        tiled=True,
    )


def after(array, earlier):
    return lax.optimization_barrier((array, earlier))[0]


def to_ring(block):
    return jnp.broadcast_to(block[None], (RING,) + block.shape)


def by_columns(arrays):
    rows = jnp.concatenate(arrays)
    n, d = rows.shape
    return rows.reshape(n, RING, d // RING).transpose(1, 0, 2)


def rows_of(*pieces):
    return jnp.concatenate([piece.reshape(-1, piece.shape[-1]) for piece in pieces])


def normalize(inputs):
    widened = inputs.astype(jnp.float32)
    inverse_rms = lax.rsqrt(jnp.mean(widened * widened, axis=-1, keepdims=True) + eps)
    return (widened * inverse_rms, inverse_rms)


def product(spec, left, right):
    return jnp.einsum(spec, left, right, preferred_element_type=jnp.float32)


def token_order():
    half = lax.axis_index("tensor") % 2
    halves = jnp.stack([half, 1 - half])
    rows = jnp.arange(RING, dtype=jnp.int32)
    within = jnp.arange(ROWS, dtype=jnp.int32)
    lanes = rows[None, :] * 2 + halves[:, None]
    return (lanes[:, :, None] * ROWS + within[None, None, :]).reshape(-1)


def segment_mask(segment_row, order):
    by_half = segment_row.reshape(RING, 2, ROWS).transpose(1, 0, 2)
    half = lax.axis_index("tensor") % 2
    segments = jnp.where(half == 0, by_half, by_half[::-1]).reshape(-1)
    causal = order[:, None] >= order[None, :]
    same_segment = segments[:, None] == segments[None, :]
    allowed = jnp.logical_and(causal, same_segment)
    return (
        allowed.astype(jnp.bfloat16),
        jnp.sum(allowed.astype(jnp.float32), axis=1, keepdims=True),
    )


def ring_sum(parts):
    return jnp.sum(parts.astype(jnp.float32), axis=0)


def mixed_of(sums, masks):
    values = sums.astype(jnp.bfloat16)
    tokens = values.shape[0] // 2
    return jnp.concatenate(
        [
            (
                jnp.dot(
                    allowed,
                    values[job * tokens : (job + 1) * tokens],
                    preferred_element_type=jnp.float32,
                )
                / counts
            ).astype(jnp.bfloat16)
            for job, (allowed, counts) in enumerate(masks)
        ]
    )


def home(sums):
    by_half = sums.reshape(2, 2, RING, ROWS, -1)
    down = by_half[0, 0] + moved(by_half[0, 1].astype(jnp.bfloat16), stay, 1).astype(jnp.float32)
    up16 = by_half[1].astype(jnp.bfloat16)
    up = moved(up16[0], mirror).astype(jnp.float32) + moved(up16[1], mirror, 1).astype(jnp.float32)
    return jnp.concatenate([down, up], axis=1)


def local(
    down_prev,
    up_prev,
    down_stash,
    up_stash,
    down_cot,
    up_cot,
    boundary,
    segment_ids,
    value_weight,
    output_weight,
):
    rank = lax.axis_index("pipe")
    is_first = rank == 0
    is_last = rank == RANKS - 1
    order = token_order()

    send_down = jnp.where(is_last, boundary[0], down_prev[0])
    send_up = jnp.where(is_first, boundary[1], up_prev[0])
    send_down_cot = jnp.where(is_first, boundary[2], down_cot[0])
    send_up_cot = jnp.where(is_last, boundary[3], up_cot[0])
    head, width = output_weight.shape[2:]
    part = width // RING

    mirrored_ids = moved(segment_ids[:, 0], mirror)

    from_below = moved(jnp.concatenate([send_down, send_up_cot]), up_one)
    from_above = moved(jnp.concatenate([send_up, send_down_cot]), down_one)
    down_in, up_g_own = from_below[:ROWS], from_below[ROWS:]
    up_in, down_g_own = from_above[:ROWS], from_above[ROWS:]

    cots = turned(by_columns([send_down_cot, send_up_cot]))
    down_g, up_g = cots[:, :ROWS], cots[:, ROWS:]
    grad_rows = rows_of(
        moved(down_g, down_one),
        moved(down_g, down_one, 1),
        moved(up_g, mirror_next),
        moved(up_g, mirror_next, 1),
    )

    down_normed, down_inverse = normalize(down_stash[0])
    up_normed, up_inverse = normalize(up_stash[0])
    normed = [normalize(down_in)[0], normalize(up_in)[0], down_normed, up_normed]
    sent = turned(
        after(
            by_columns([n.astype(jnp.bfloat16) for n in normed] + [output_weight[0, 0]]), cots
        )
    )
    down_x, up_x, down_n, up_n = (sent[:, i * ROWS : (i + 1) * ROWS] for i in range(4))
    output_cols = sent[:, 4 * ROWS :]
    forward_rows = rows_of(down_x, moved(down_x, stay, 1), moved(up_x, mirror), moved(up_x, mirror, 1))
    kept_rows = rows_of(down_n, moved(down_n, stay, 1), moved(up_n, mirror), moved(up_n, mirror, 1))

    forward_masks = (
        segment_mask(segment_ids[0, 0], order),
        segment_mask(mirrored_ids[1], order),
    )
    backward_masks = (
        segment_mask(segment_ids[2, 0], order),
        segment_mask(mirrored_ids[3], order),
    )

    scaled_parts = product("rd,hkd->hrk", grad_rows, output_cols).astype(jnp.bfloat16)
    got = turned(
        after(
            jnp.concatenate([value_weight[0, 0].reshape(RING, part, head), scaled_parts], axis=1),
            sent,
        )
    )
    value_cols, scaled = got[:, :part], ring_sum(got[:, part:])
    tokens = scaled.shape[0] // 2
    act = jnp.concatenate(
        [
            contract_rows(
                allowed,
                (scaled[job * tokens : (job + 1) * tokens] / counts).astype(jnp.bfloat16),
            ).astype(jnp.bfloat16)
            for job, (allowed, counts) in enumerate(backward_masks)
        ]
    )

    forward_parts = product("rd,hdk->hrk", forward_rows, value_cols).astype(jnp.bfloat16)
    got = turned(jnp.concatenate([to_ring(act), forward_parts], axis=1))
    acts, forward_values = got[:, : 2 * tokens], ring_sum(got[:, 2 * tokens :])
    normed_grads = home(product("hrk,hdk->rd", acts, value_cols))

    forward_mixed = mixed_of(forward_values, forward_masks)
    kept_parts = product("rd,hdk->hrk", kept_rows, value_cols).astype(jnp.bfloat16)
    got = turned(jnp.concatenate([to_ring(forward_mixed), kept_parts], axis=1))
    forward_mixes, kept_values = got[:, : 2 * tokens], ring_sum(got[:, 2 * tokens :])
    added = home(product("hrk,hkd->rd", forward_mixes, output_cols))

    kept_mixed = mixed_of(kept_values, backward_masks)
    value_grad = product("rd,hrk->hdk", kept_rows, acts).astype(jnp.bfloat16)
    got = turned(jnp.concatenate([to_ring(kept_mixed), value_grad], axis=1))
    kept_mixes, value_grad = got[:, : 2 * tokens], got[:, 2 * tokens :]

    output_grad = product("hrk,rd->hkd", kept_mixes, grad_rows)
    got = turned(jnp.concatenate([normed_grads, added, output_grad], axis=1).astype(jnp.bfloat16))
    output_grad = got[:, 4 * ROWS :]
    back = got[:, : 4 * ROWS].astype(jnp.float32)
    back = back.reshape(RING, 4, ROWS, part).transpose(1, 2, 0, 3).reshape(4, ROWS, width)

    def input_grad(own_grad, own_normed, own_inverse, normed_grad):
        project = jnp.mean(normed_grad * own_normed, axis=-1, keepdims=True)
        out = own_grad.astype(jnp.float32) + own_inverse * (normed_grad - own_normed * project)
        return out.astype(jnp.bfloat16)

    down_back = input_grad(down_g_own, down_normed, down_inverse, back[0])
    up_back = input_grad(up_g_own, up_normed, up_inverse, back[1])
    down_out = (down_in.astype(jnp.float32) + back[2]).astype(jnp.bfloat16)
    up_out = (up_in.astype(jnp.float32) + back[3]).astype(jnp.bfloat16)

    return (
        down_out[None],
        up_out[None],
        down_back[None],
        up_back[None],
        value_grad.reshape(width, head).astype(jnp.float32)[None],
        output_grad.transpose(1, 0, 2).reshape(head, width).astype(jnp.float32)[None],
    )


def contract_rows(left, right):
    return lax.dot_general(
        left, right, (((0,), (0,)), ((), ())), preferred_element_type=jnp.float32
    )


def solution(mesh):
    placed = (
        P("pipe", "tensor", None),
        P("pipe", "tensor", None),
        P("pipe", "tensor", None),
        P("pipe", "tensor", None),
        P("pipe", "tensor", None),
        P("pipe", "tensor", None),
        P(None, "tensor", None),
        P(None, "pipe", None),
        P("pipe", None, None, "tensor"),
        P("pipe", None, "tensor", None),
    )
    return jax.shard_map(
        local,
        mesh=mesh,
        in_specs=placed,
        out_specs=(
            P("pipe", "tensor", None),
            P("pipe", "tensor", None),
            P("pipe", "tensor", None),
            P("pipe", "tensor", None),
            P("pipe", None, "tensor"),
            P("pipe", "tensor", None),
        ),
        check_vma=False,
    )
```

```python
import jax
import jax.numpy as jnp
from jax import lax
from jax.experimental import pallas as pl
from jax.experimental.pallas import tpu as pltpu
from jax.sharding import PartitionSpec as P

eps = 1e-05

RANKS = 32
LANES = 8
RING = 4
ROWS = 32
HALF = RING * ROWS
TOKENS = 2 * HALF
HEAD = 128
WIDTH = 4096
PART = WIDTH // RING
BF16 = jnp.bfloat16
F32 = jnp.float32


def spot(rank, row, half):
    return (rank % RANKS) * LANES + (row % RING) * 2 + half % 2


def moved(shard, rank_to, half_by=0):
    pairs = [
        (spot(r, y, z), spot(rank_to(r), y, z + half_by))
        for r in range(RANKS)
        for y in range(RING)
        for z in range(2)
    ]
    return lax.ppermute(shard, ("pipe", "tensor"), pairs)


def stay(r):
    return r


def up_one(r):
    return r + 1


def down_one(r):
    return r - 1


def mirror(r):
    return RANKS - 1 - r


def mirror_next(r):
    return RANKS - 2 - r


def turned(blocks):
    return lax.all_to_all(
        blocks,
        "tensor",
        split_axis=0,
        concat_axis=0,
        axis_index_groups=[[0, 2, 4, 6], [1, 3, 5, 7]],
        tiled=True,
    )


def after(array, earlier):
    return lax.optimization_barrier((array, earlier))[0]


def block(shape, *index):
    return pl.BlockSpec(shape, lambda i: index)


def whole(array):
    rank = array.ndim
    return pl.BlockSpec(array.shape, lambda i: (0,) * rank)


SCALARS = pl.BlockSpec(memory_space=pltpu.SMEM)


def run(kernel, outs, operands, filled=None, beside=False):
    pairs = [o if isinstance(o, tuple) else (o, whole(o)) for o in operands]
    outs = [o if isinstance(o, tuple) else (o, whole(o)) for o in outs]
    body = kernel
    if filled is not None:
        pairs = [(filled, pl.BlockSpec(memory_space=pl.ANY))] + pairs

        def body(_, *refs):
            kernel(*refs)

    return pl.pallas_call(
        body,
        grid=(1,),
        out_shape=[o for o, _ in outs],
        in_specs=[spec for _, spec in pairs],
        out_specs=[spec for _, spec in outs],
        input_output_aliases={} if filled is None else {0: 0},
        compiler_params=pltpu.CompilerParams(vmem_limit_bytes=63 * 1024 * 1024),
        cost_estimate=pl.CostEstimate(
            flops=10**11 if beside else 1, bytes_accessed=1, transcendentals=0
        ),
    )(*[array for array, _ in pairs])


def out(shape, dtype=BF16):
    return jax.ShapeDtypeStruct(shape, dtype)


def dot(left, right, left_dim=1, right_dim=0):
    return lax.dot_general(
        left, right, (((left_dim,), (right_dim,)), ((), ())), preferred_element_type=F32
    )


def inverse_of(x):
    return lax.rsqrt(jnp.mean(x * x, axis=-1, keepdims=True) + eps)


def columns(ref, row, count, rows):
    for q in range(RING):
        ref[q, row : row + count, :] = rows[:, q * PART : (q + 1) * PART]


def flat(ref):
    return ref[...].reshape(HALF, PART)


def heads(ref):
    return jnp.concatenate([ref[h] for h in range(RING)], axis=1)


def send_kernel(
    place,
    down_prev,
    up_prev,
    down_stash,
    up_stash,
    down_cot,
    up_cot,
    boundary,
    up_ids,
    output_weight,
    below,
    above,
    down_normed,
    up_normed,
    cots,
):
    for stash, normed in ((down_stash, down_normed), (up_stash, up_normed)):
        x = stash[0].astype(F32)
        normed[:, :WIDTH] = (x * inverse_of(x)).astype(BF16)
    up_normed[:, WIDTH:] = up_ids[...]
    columns(cots, 0, HEAD, output_weight[0, 0])
    first = place[0] == 0
    last = place[0] == RANKS - 1

    def choose(edge, index, usual, ref, row, columns_row=None):
        def write(rows):
            ref[row : row + ROWS, :] = rows
            if columns_row is not None:
                columns(cots, columns_row, ROWS, rows)

        @pl.when(edge)
        def _():
            write(boundary[index])

        @pl.when(jnp.logical_not(edge))
        def _():
            write(usual[0])

    choose(last, 0, down_prev, below, 0)
    choose(last, 3, up_cot, below, ROWS, HEAD + ROWS)
    choose(first, 1, up_prev, above, 0)
    choose(first, 2, down_cot, above, ROWS, HEAD)


def inputs_kernel(below, above, n0, n1, n2, n3, sent):
    for i, rows in enumerate((below, above)):
        x = rows[...].astype(F32)
        columns(sent, i * ROWS, ROWS, (x * inverse_of(x)).astype(BF16))
    for i, rows in enumerate((n0, n1, n2, n3)):
        columns(sent, (2 + i) * ROWS, ROWS, rows[:, :WIDTH])


def value_in_kernel(value_weight, sums):
    for q in range(RING):
        sums[q] = value_weight[0, 0, q * PART : (q + 1) * PART, :]


def scaled_kernel(g0, g1, g2, g3, output_cols, sums):
    weights = output_cols[...].reshape(RING * HEAD, PART)
    for i, g in enumerate((g0, g1, g2, g3)):
        parts = dot(flat(g), weights, 1, 1).astype(BF16)
        for h in range(RING):
            sums[h, i * HALF : (i + 1) * HALF, :] = parts[:, h * HEAD : (h + 1) * HEAD]


def token_of(place, dim):
    i = lax.broadcasted_iota(jnp.int32, (TOKENS, TOKENS), dim)
    half = ((i >> 7) + place[1]) & 1
    return (((i >> 5) & 3) * 2 + half) * ROWS + (i & 31)


def mask_kernel(place, ids_row, ids_col, allowed, back):
    rows, cols = token_of(place, 0), token_of(place, 1)
    for job in range(4):
        same = ids_col[:, job : job + 1] == ids_row[job : job + 1, :]
        allowed[job] = jnp.where(jnp.logical_and(rows >= cols, same), 1.0, 0.0).astype(BF16)
        if job >= 2:
            back[job - 2] = jnp.where(jnp.logical_and(cols >= rows, same), 1.0, 0.0).astype(BF16)


def counts_of(allowed):
    return jnp.sum(allowed.astype(F32), axis=1, keepdims=True)


def ring_sum(ref, job):
    rows = slice(job * TOKENS, (job + 1) * TOKENS)
    total = ref[0, rows, :].astype(F32)
    for h in range(1, RING):
        total = total + ref[h, rows, :].astype(F32)
    return total


def act_kernel(allowed, back, sums, acts):
    for job in range(2):
        scaled = (ring_sum(sums, job) / counts_of(allowed[2 + job])).astype(BF16)
        act = dot(back[job], scaled).astype(BF16)
        for h in range(RING):
            acts[h, job * TOKENS : (job + 1) * TOKENS, :] = act


def value_parts(pieces, value_cols, ref, row):
    rows = jnp.concatenate([flat(piece) for piece in pieces], axis=0)
    for h in range(RING):
        ref[h, row : row + 2 * TOKENS, :] = dot(rows, value_cols[h]).astype(BF16)


def values_kernel(x0, x1, x2, x3, value_cols, sums):
    value_parts((x0, x1, x2, x3), value_cols, sums, 0)


def split_home(total, down_own, down_other, up_own, up_other):
    for i, ref in enumerate((down_own, down_other, up_own, up_other)):
        piece = total[i * HALF : (i + 1) * HALF, :].reshape(RING, ROWS, PART)
        ref[...] = piece.astype(ref.dtype)


def normed_grad_kernel(acts, value_cols, *refs):
    split_home(dot(heads(acts), heads(value_cols), 1, 1), *refs)


def added_kernel(mixes, output_cols, *refs):
    weights = output_cols[...].reshape(RING * HEAD, PART)
    split_home(dot(heads(mixes), weights), *refs)


def mixed_kernel(allowed, first, second, mixes):
    for job in range(4):
        values = first if job < 2 else second
        summed = ring_sum(values, job % 2).astype(BF16)
        mix = (dot(allowed[job], summed) / counts_of(allowed[job])).astype(BF16)
        for h in range(RING):
            mixes[h, job * TOKENS : (job + 1) * TOKENS, :] = mix


def grad_kernel(p0, p1, p2, p3, acts, sums):
    rows = jnp.concatenate([flat(piece) for piece in (p0, p1, p2, p3)], axis=0)
    grad = dot(heads(acts), rows, 0, 0).astype(BF16)
    sums[...] = grad.reshape(RING, HEAD, PART)


def sum_kernel(own, other, up_own, up_other, sums):
    sums[:, :ROWS, :] = (own[...] + other[...].astype(F32)).astype(BF16)
    sums[:, ROWS:, :] = (up_own[...].astype(F32) + up_other[...].astype(F32)).astype(BF16)


def value_out_kernel(got, grad):
    for q in range(RING):
        grad[0, q * PART : (q + 1) * PART, :] = got[q].astype(F32).T


def output_out_kernel(got, grad):
    for q in range(RING):
        grad[0, :, q * PART : (q + 1) * PART] = got[q].astype(F32)


def rows_at(got, row):
    return jnp.concatenate([got[q, row : row + ROWS, :] for q in range(RING)], axis=1).astype(F32)


def backward_out_kernel(got, down_grad, up_grad, down_stash, up_stash, down_back, up_back):
    for i, (own_grad, stash, back) in enumerate(
        ((down_grad, down_stash, down_back), (up_grad, up_stash, up_back))
    ):
        normed_grad = rows_at(got, i * ROWS)
        x = stash[0].astype(F32)
        inverse = inverse_of(x)
        normed = x * inverse
        project = jnp.mean(normed_grad * normed, axis=-1, keepdims=True)
        back[0] = (
            own_grad[...].astype(F32) + inverse * (normed_grad - normed * project)
        ).astype(BF16)


def forward_out_kernel(got, down_in, up_in, down_out, up_out):
    down_out[0] = (down_in[...].astype(F32) + rows_at(got, 0)).astype(BF16)
    up_out[0] = (up_in[...].astype(F32) + rows_at(got, ROWS)).astype(BF16)


def home(pieces):
    own, other, up_own, up_other = pieces
    return own, moved(other, stay, 1), moved(up_own, mirror), moved(up_other, mirror, 1)


def local(
    down_prev,
    up_prev,
    down_stash,
    up_stash,
    down_cot,
    up_cot,
    boundary,
    segment_ids,
    value_weight,
    output_weight,
):
    half = lax.axis_index("tensor") % 2
    place = jnp.stack([lax.axis_index("pipe"), half]).astype(jnp.int32)
    placed = (place, SCALARS)
    rows32 = (ROWS, WIDTH)
    cols32 = (RING, ROWS, PART)

    wide = (RING, PART + 2 * TOKENS, HEAD)
    wide_first = block((RING, PART, HEAD), 0, 0, 0)
    wide_last = block((RING, 2 * TOKENS, HEAD), 0, 2, 0)
    lower = block((RING, 2 * TOKENS, HEAD), 0, 0, 0)
    upper = block((RING, 2 * TOKENS, HEAD), 0, 1, 0)

    wide = out((RING, PART + 2 * TOKENS, HEAD))
    narrow, double = out((RING, 2 * TOKENS, HEAD)), out((RING, 4 * TOKENS, HEAD))
    lower, upper, last = (block((RING, 2 * TOKENS, HEAD), 0, i, 0) for i in range(3))
    first = block((RING, PART, HEAD), 0, 0, 0)

    up_ids = jnp.pad(segment_ids[1::2, 0].reshape(4, HEAD), ((0, ROWS - 4), (0, 0))).astype(BF16)

    below_sent, above_sent, down_n, up_n, cots = run(
        send_kernel,
        [
            out((2 * ROWS, WIDTH)),
            out((2 * ROWS, WIDTH)),
            out(rows32),
            out((ROWS, WIDTH + HEAD)),
            out((RING, HEAD + 2 * ROWS, PART)),
        ],
        [
            placed,
            down_prev,
            up_prev,
            down_stash,
            up_stash,
            down_cot,
            up_cot,
            boundary,
            up_ids,
            (output_weight, block((1, 1, HEAD, WIDTH), 0, 0, 0, 0)),
        ],
    )
    kept_rows = (down_n, moved(down_n, stay, 1), moved(up_n, mirror), moved(up_n, mirror, 1))
    below = moved(below_sent, up_one)
    above = moved(above_sent, down_one)

    cots = turned(cots)
    output_cols = (cots, block((RING, HEAD, PART), 0, 0, 0))
    down_g, up_g = cots[:, HEAD : HEAD + ROWS], cots[:, HEAD + ROWS :]
    grads = (
        moved(down_g, down_one),
        moved(down_g, down_one, 1),
        moved(up_g, mirror_next),
        moved(up_g, mirror_next, 1),
    )

    sent = run(
        inputs_kernel,
        [out((RING, 6 * ROWS, PART))],
        [(below, block(rows32, 0, 0)), (above, block(rows32, 0, 0)), *kept_rows],
    )[0]
    sent = turned(after(sent, cots))
    kept = [(sent, block(cols32, 0, 2 + i, 0)) for i in range(4)]
    down_x, up_x = sent[:, :ROWS], sent[:, ROWS : 2 * ROWS]
    inputs = (
        (sent, block(cols32, 0, 0, 0)),
        moved(down_x, stay, 1),
        moved(up_x, mirror),
        moved(up_x, mirror, 1),
    )

    mirrored = kept_rows[2][:4, WIDTH:].astype(jnp.int32).reshape(2, TOKENS)
    ids = jnp.stack([segment_ids[0, 0], mirrored[0], segment_ids[2, 0], mirrored[1]])
    by_half = ids.reshape(4, RING, 2, ROWS).transpose(0, 2, 1, 3)
    ids_row = jnp.where(half == 0, by_half, by_half[:, ::-1]).reshape(4, TOKENS)
    ids_col = ids_row.T
    square = (TOKENS, TOKENS)
    allowed, allowed_back = run(
        mask_kernel, [out((4, *square)), out((2, *square))], [placed, ids_row, ids_col], beside=True
    )

    got3 = run(
        value_in_kernel,
        [(wide, first)],
        [(after(value_weight, cots), block((1, 1, WIDTH, HEAD), 0, 0, 0, 0))],
        beside=True,
    )[0]
    got3 = run(scaled_kernel, [(wide, last)], [*grads, output_cols], filled=got3)[0]
    got3 = turned(after(got3, sent))
    value_cols = (got3, first)

    acts = run(act_kernel, [narrow], [allowed, allowed_back, (got3, last)])[0]
    acts = turned(after(acts, inputs[1:]))
    pieces = [out(cols32, F32), out(cols32), out(cols32), out(cols32)]
    normed_grads = run(normed_grad_kernel, pieces, [acts, value_cols])
    ready = normed_grads[1]
    normed_grads = home(normed_grads)

    values = run(values_kernel, [(double, upper)], [*kept, value_cols])[0]
    values = after(values, ready)
    values = turned(
        run(values_kernel, [(double, lower)], [*inputs, value_cols], filled=values)[0]
    )

    mixes = turned(run(mixed_kernel, [double], [allowed, (values, lower), (values, upper)])[0])
    added = run(added_kernel, pieces, [(mixes, lower), output_cols])
    ready = added[1]
    added = home(added)

    tall = out((RING, 2 * HEAD + 2 * ROWS, PART))
    value_part, output_part = (block((RING, HEAD, PART), 0, i, 0) for i in range(2))
    rows_part = block((RING, 2 * ROWS, PART), 0, 4, 0)
    sums = run(grad_kernel, [(tall, value_part)], [*kept, acts], beside=True)[0]
    sums = run(sum_kernel, [(tall, rows_part)], [*normed_grads], filled=sums, beside=True)[0]
    sums = turned(
        run(
            grad_kernel,
            [(tall, output_part)],
            [*grads, (after(mixes, ready), upper)],
            filled=sums,
        )[0]
    )
    value_grad = run(value_out_kernel, [out((1, WIDTH, HEAD), F32)], [(sums, value_part)])[0]
    output_grad = run(output_out_kernel, [out((1, HEAD, WIDTH), F32)], [(sums, output_part)])[0]
    lower_rows, upper_rows = (block(rows32, i, 0) for i in range(2))
    down_back, up_back = run(
        backward_out_kernel,
        [out((1, ROWS, WIDTH))] * 2,
        [(sums, rows_part), (above, upper_rows), (below, upper_rows), down_stash, up_stash],
    )

    rows = turned(after(run(sum_kernel, [out((RING, 2 * ROWS, PART))], [*added])[0], sums))
    down_out, up_out = run(
        forward_out_kernel,
        [out((1, ROWS, WIDTH))] * 2,
        [rows, (below, lower_rows), (above, lower_rows)],
    )
    return down_out, up_out, down_back, up_back, value_grad, output_grad


def solution(mesh):
    placed = (
        P("pipe", "tensor", None),
        P("pipe", "tensor", None),
        P("pipe", "tensor", None),
        P("pipe", "tensor", None),
        P("pipe", "tensor", None),
        P("pipe", "tensor", None),
        P(None, "tensor", None),
        P(None, "pipe", None),
        P("pipe", None, None, "tensor"),
        P("pipe", None, "tensor", None),
    )
    return jax.shard_map(
        local,
        mesh=mesh,
        in_specs=placed,
        out_specs=(
            P("pipe", "tensor", None),
            P("pipe", "tensor", None),
            P("pipe", "tensor", None),
            P("pipe", "tensor", None),
            P("pipe", None, "tensor"),
            P("pipe", "tensor", None),
        ),
        check_vma=False,
    )
```

```python
import jax
import jax.numpy as jnp
from jax import lax
from jax.experimental import pallas as pl
from jax.experimental.pallas import tpu as pltpu
from jax.sharding import PartitionSpec as P

eps = 1e-05

RANKS = 32
LANES = 8
RING = 4
ROWS = 32
HALF = RING * ROWS
TOKENS = 2 * HALF
HEAD = 128
WIDTH = 4096
PART = WIDTH // RING
BF16 = jnp.bfloat16
F32 = jnp.float32


def spot(rank, row, half):
    return (rank % RANKS) * LANES + (row % RING) * 2 + half % 2


def moved(shard, rank_to, half_by=0):
    pairs = [
        (spot(r, y, z), spot(rank_to(r), y, z + half_by))
        for r in range(RANKS)
        for y in range(RING)
        for z in range(2)
    ]
    return lax.ppermute(shard, ("pipe", "tensor"), pairs)


def stay(r):
    return r


def up_one(r):
    return r + 1


def down_one(r):
    return r - 1


def mirror(r):
    return RANKS - 1 - r


def mirror_next(r):
    return RANKS - 2 - r


def turned(blocks):
    return lax.all_to_all(
        blocks,
        "tensor",
        split_axis=0,
        concat_axis=0,
        axis_index_groups=[[0, 2, 4, 6], [1, 3, 5, 7]],
        tiled=True,
    )


def after(array, earlier):
    return lax.optimization_barrier((array, earlier))[0]


def block(shape, *index):
    return pl.BlockSpec(shape, lambda i: index)


def whole(array):
    rank = array.ndim
    return pl.BlockSpec(array.shape, lambda i: (0,) * rank)


SCALARS = pl.BlockSpec(memory_space=pltpu.SMEM)


def run(kernel, outs, operands, filled=None, beside=False):
    pairs = [o if isinstance(o, tuple) else (o, whole(o)) for o in operands]
    outs = [o if isinstance(o, tuple) else (o, whole(o)) for o in outs]
    body = kernel
    if filled is not None:
        pairs = [(filled, pl.BlockSpec(memory_space=pl.ANY))] + pairs

        def body(_, *refs):
            kernel(*refs)

    return pl.pallas_call(
        body,
        grid=(1,),
        out_shape=[o for o, _ in outs],
        in_specs=[spec for _, spec in pairs],
        out_specs=[spec for _, spec in outs],
        input_output_aliases={} if filled is None else {0: 0},
        compiler_params=pltpu.CompilerParams(vmem_limit_bytes=63 * 1024 * 1024),
        cost_estimate=pl.CostEstimate(
            flops=10**11 if beside else 1, bytes_accessed=1, transcendentals=0
        ),
    )(*[array for array, _ in pairs])


def out(shape, dtype=BF16):
    return jax.ShapeDtypeStruct(shape, dtype)


def dot(left, right, left_dim=1, right_dim=0):
    return lax.dot_general(
        left, right, (((left_dim,), (right_dim,)), ((), ())), preferred_element_type=F32
    )


def inverse_of(x):
    return lax.rsqrt(jnp.mean(x * x, axis=-1, keepdims=True) + eps)


def columns(ref, row, count, rows):
    for q in range(RING):
        ref[q, row : row + count, :] = rows[:, q * PART : (q + 1) * PART]


def flat(ref):
    return ref[...].reshape(HALF, PART)


def heads(ref):
    return jnp.concatenate([ref[h] for h in range(RING)], axis=1)


def send_kernel(
    place,
    down_prev,
    up_prev,
    down_stash,
    up_stash,
    down_cot,
    up_cot,
    boundary,
    up_ids,
    output_weight,
    below,
    above,
    down_normed,
    up_normed,
    cots,
):
    for stash, normed in ((down_stash, down_normed), (up_stash, up_normed)):
        x = stash[0].astype(F32)
        normed[:, :WIDTH] = (x * inverse_of(x)).astype(BF16)
    ids = [up_ids[job, :, i * HEAD : (i + 1) * HEAD] for job in (1, 3) for i in range(2)]
    ids.append(jnp.zeros((ROWS - 4, HEAD), jnp.int32))
    up_normed[:, WIDTH:] = jnp.concatenate(ids, axis=0).astype(F32).astype(BF16)
    columns(cots, 0, HEAD, output_weight[0, 0])
    first = place[0] == 0
    last = place[0] == RANKS - 1

    def choose(edge, index, usual, ref, row, columns_row=None):
        def write(rows):
            ref[row : row + ROWS, :] = rows
            if columns_row is not None:
                columns(cots, columns_row, ROWS, rows)

        @pl.when(edge)
        def _():
            write(boundary[index])

        @pl.when(jnp.logical_not(edge))
        def _():
            write(usual[0])

    choose(last, 0, down_prev, below, 0)
    choose(last, 3, up_cot, below, ROWS, HEAD + ROWS)
    choose(first, 1, up_prev, above, 0)
    choose(first, 2, down_cot, above, ROWS, HEAD)


def inputs_kernel(below, above, n0, n1, n2, n3, sent):
    for i, rows in enumerate((below, above)):
        x = rows[...].astype(F32)
        columns(sent, i * ROWS, ROWS, (x * inverse_of(x)).astype(BF16))
    for i, rows in enumerate((n0, n1, n2, n3)):
        columns(sent, (2 + i) * ROWS, ROWS, rows[:, :WIDTH])


def value_in_kernel(value_weight, sums):
    for q in range(RING):
        sums[q] = value_weight[0, 0, q * PART : (q + 1) * PART, :]


def scaled_kernel(g0, g1, g2, g3, output_cols, sums):
    weights = output_cols[...].reshape(RING * HEAD, PART)
    for i, g in enumerate((g0, g1, g2, g3)):
        parts = dot(flat(g), weights, 1, 1).astype(BF16)
        for h in range(RING):
            sums[h, i * HALF : (i + 1) * HALF, :] = parts[:, h * HEAD : (h + 1) * HEAD]


def token_of(place, dim):
    i = lax.broadcasted_iota(jnp.int32, (TOKENS, TOKENS), dim)
    half = ((i >> 7) + place[1]) & 1
    return (((i >> 5) & 3) * 2 + half) * ROWS + (i & 31)


def mask_kernel(place, ids_row, ids_col, allowed, back):
    rows, cols = token_of(place, 0), token_of(place, 1)
    for job in range(4):
        same = ids_col[:, job : job + 1] == ids_row[job : job + 1, :]
        allowed[job] = jnp.where(jnp.logical_and(rows >= cols, same), 1.0, 0.0).astype(BF16)
        if job >= 2:
            back[job - 2] = jnp.where(jnp.logical_and(cols >= rows, same), 1.0, 0.0).astype(BF16)


def counts_of(allowed):
    return jnp.sum(allowed.astype(F32), axis=1, keepdims=True)


def ring_sum(ref, job):
    rows = slice(job * TOKENS, (job + 1) * TOKENS)
    total = ref[0, rows, :].astype(F32)
    for h in range(1, RING):
        total = total + ref[h, rows, :].astype(F32)
    return total


def act_kernel(allowed, back, sums, acts):
    for job in range(2):
        scaled = (ring_sum(sums, job) / counts_of(allowed[2 + job])).astype(BF16)
        act = dot(back[job], scaled).astype(BF16)
        for h in range(RING):
            acts[h, job * TOKENS : (job + 1) * TOKENS, :] = act


def value_parts(pieces, value_cols, ref, row):
    rows = jnp.concatenate([flat(piece) for piece in pieces], axis=0)
    for h in range(RING):
        ref[h, row : row + 2 * TOKENS, :] = dot(rows, value_cols[h]).astype(BF16)


def values_kernel(x0, x1, x2, x3, value_cols, sums):
    value_parts((x0, x1, x2, x3), value_cols, sums, 0)


def split_home(total, down_own, down_other, up_own, up_other):
    for i, ref in enumerate((down_own, down_other, up_own, up_other)):
        piece = total[i * HALF : (i + 1) * HALF, :].reshape(RING, ROWS, PART)
        ref[...] = piece.astype(ref.dtype)


def normed_grad_kernel(acts, value_cols, *refs):
    split_home(dot(heads(acts), heads(value_cols), 1, 1), *refs)


def added_kernel(mixes, output_cols, *refs):
    weights = output_cols[...].reshape(RING * HEAD, PART)
    split_home(dot(heads(mixes), weights), *refs)


def mixed_kernel(allowed, first, second, mixes):
    for job in range(4):
        values = first if job < 2 else second
        summed = ring_sum(values, job % 2).astype(BF16)
        mix = (dot(allowed[job], summed) / counts_of(allowed[job])).astype(BF16)
        for h in range(RING):
            mixes[h, job * TOKENS : (job + 1) * TOKENS, :] = mix


def grad_kernel(p0, p1, p2, p3, acts, sums):
    rows = jnp.concatenate([flat(piece) for piece in (p0, p1, p2, p3)], axis=0)
    grad = dot(heads(acts), rows, 0, 0).astype(BF16)
    sums[...] = grad.reshape(RING, HEAD, PART)


def added_grad_kernel(mixes, output_cols, g0, g1, g2, g3, kept_mixes, sums, *refs):
    added_kernel(mixes, output_cols, *refs)
    grad_kernel(g0, g1, g2, g3, kept_mixes, sums)


def sum_kernel(own, other, up_own, up_other, sums):
    sums[:, :ROWS, :] = (own[...] + other[...].astype(F32)).astype(BF16)
    sums[:, ROWS:, :] = (up_own[...].astype(F32) + up_other[...].astype(F32)).astype(BF16)


def value_out_kernel(got, grad):
    for q in range(RING):
        grad[0, q * PART : (q + 1) * PART, :] = got[q].astype(F32).T


def output_out_kernel(got, grad):
    for q in range(RING):
        grad[0, :, q * PART : (q + 1) * PART] = got[q].astype(F32)


def rows_at(got, row):
    return jnp.concatenate([got[q, row : row + ROWS, :] for q in range(RING)], axis=1).astype(F32)


def backward_out_kernel(got, down_grad, up_grad, down_stash, up_stash, down_back, up_back):
    for i, (own_grad, stash, back) in enumerate(
        ((down_grad, down_stash, down_back), (up_grad, up_stash, up_back))
    ):
        normed_grad = rows_at(got, i * ROWS)
        x = stash[0].astype(F32)
        inverse = inverse_of(x)
        normed = x * inverse
        project = jnp.mean(normed_grad * normed, axis=-1, keepdims=True)
        back[0] = (
            own_grad[...].astype(F32) + inverse * (normed_grad - normed * project)
        ).astype(BF16)


def forward_out_kernel(got, down_in, up_in, down_out, up_out):
    down_out[0] = (down_in[...].astype(F32) + rows_at(got, 0)).astype(BF16)
    up_out[0] = (up_in[...].astype(F32) + rows_at(got, ROWS)).astype(BF16)


def home(pieces):
    own, other, up_own, up_other = pieces
    return own, moved(other, stay, 1), moved(up_own, mirror), moved(up_other, mirror, 1)


def local(
    down_prev,
    up_prev,
    down_stash,
    up_stash,
    down_cot,
    up_cot,
    boundary,
    segment_ids,
    value_weight,
    output_weight,
):
    half = lax.axis_index("tensor") % 2
    place = jnp.stack([lax.axis_index("pipe"), half]).astype(jnp.int32)
    placed = (place, SCALARS)
    rows32 = (ROWS, WIDTH)
    cols32 = (RING, ROWS, PART)

    wide = (RING, PART + 2 * TOKENS, HEAD)
    wide_first = block((RING, PART, HEAD), 0, 0, 0)
    wide_last = block((RING, 2 * TOKENS, HEAD), 0, 2, 0)
    lower = block((RING, 2 * TOKENS, HEAD), 0, 0, 0)
    upper = block((RING, 2 * TOKENS, HEAD), 0, 1, 0)

    wide = out((RING, PART + 2 * TOKENS, HEAD))
    narrow, double = out((RING, 2 * TOKENS, HEAD)), out((RING, 4 * TOKENS, HEAD))
    lower, upper, last = (block((RING, 2 * TOKENS, HEAD), 0, i, 0) for i in range(3))
    first = block((RING, PART, HEAD), 0, 0, 0)

    below_sent, above_sent, down_n, up_n, cots = run(
        send_kernel,
        [
            out((2 * ROWS, WIDTH)),
            out((2 * ROWS, WIDTH)),
            out(rows32),
            out((ROWS, WIDTH + HEAD)),
            out((RING, HEAD + 2 * ROWS, PART)),
        ],
        [
            placed,
            down_prev,
            up_prev,
            down_stash,
            up_stash,
            down_cot,
            up_cot,
            boundary,
            segment_ids,
            (output_weight, block((1, 1, HEAD, WIDTH), 0, 0, 0, 0)),
        ],
    )
    kept_rows = (down_n, moved(down_n, stay, 1), moved(up_n, mirror), moved(up_n, mirror, 1))
    below = moved(below_sent, up_one)
    above = moved(above_sent, down_one)

    cots = turned(cots)
    output_cols = (cots, block((RING, HEAD, PART), 0, 0, 0))
    down_g, up_g = cots[:, HEAD : HEAD + ROWS], cots[:, HEAD + ROWS :]
    grads = (
        moved(down_g, down_one),
        moved(down_g, down_one, 1),
        moved(up_g, mirror_next),
        moved(up_g, mirror_next, 1),
    )

    sent = run(
        inputs_kernel,
        [out((RING, 6 * ROWS, PART))],
        [(below, block(rows32, 0, 0)), (above, block(rows32, 0, 0)), *kept_rows],
    )[0]
    sent = turned(after(sent, cots))
    kept = [(sent, block(cols32, 0, 2 + i, 0)) for i in range(4)]
    down_x, up_x = sent[:, :ROWS], sent[:, ROWS : 2 * ROWS]
    inputs = (
        (sent, block(cols32, 0, 0, 0)),
        moved(down_x, stay, 1),
        moved(up_x, mirror),
        moved(up_x, mirror, 1),
    )

    mirrored = kept_rows[2][:4, WIDTH:].astype(jnp.int32).reshape(2, TOKENS)
    ids = jnp.stack([segment_ids[0, 0], mirrored[0], segment_ids[2, 0], mirrored[1]])
    by_half = ids.reshape(4, RING, 2, ROWS).transpose(0, 2, 1, 3)
    ids_row = jnp.where(half == 0, by_half, by_half[:, ::-1]).reshape(4, TOKENS)
    ids_col = ids_row.T
    square = (TOKENS, TOKENS)
    allowed, allowed_back = run(
        mask_kernel, [out((4, *square)), out((2, *square))], [placed, ids_row, ids_col], beside=True
    )

    got3 = run(
        value_in_kernel,
        [(wide, first)],
        [(after(value_weight, cots), block((1, 1, WIDTH, HEAD), 0, 0, 0, 0))],
        beside=True,
    )[0]
    got3 = run(scaled_kernel, [(wide, last)], [*grads, output_cols], filled=got3)[0]
    got3 = turned(after(got3, sent))
    value_cols = (got3, first)

    acts = run(act_kernel, [narrow], [allowed, allowed_back, (got3, last)])[0]
    acts = turned(after(acts, inputs[1:]))
    pieces = [out(cols32, F32), out(cols32), out(cols32), out(cols32)]
    normed_grads = run(normed_grad_kernel, pieces, [acts, value_cols])
    ready = normed_grads[1]
    normed_grads = home(normed_grads)

    values = run(values_kernel, [(double, upper)], [*kept, value_cols])[0]
    values = after(values, ready)
    values = turned(
        run(values_kernel, [(double, lower)], [*inputs, value_cols], filled=values)[0]
    )

    mixes = turned(run(mixed_kernel, [double], [allowed, (values, lower), (values, upper)])[0])
    tall = out((RING, 2 * HEAD + 2 * ROWS, PART))
    value_part, output_part = (block((RING, HEAD, PART), 0, i, 0) for i in range(2))
    rows_part = block((RING, 2 * ROWS, PART), 0, 4, 0)
    sums = run(grad_kernel, [(tall, value_part)], [*kept, acts], beside=True)[0]
    sums = run(sum_kernel, [(tall, rows_part)], [*normed_grads], filled=sums, beside=True)[0]
    sums, *added = run(
        added_grad_kernel,
        [(tall, output_part), *pieces],
        [(mixes, lower), output_cols, *grads, (mixes, upper)],
        filled=sums,
    )
    added = home(added)
    sums = turned(sums)
    value_grad = run(value_out_kernel, [out((1, WIDTH, HEAD), F32)], [(sums, value_part)])[0]
    output_grad = run(output_out_kernel, [out((1, HEAD, WIDTH), F32)], [(sums, output_part)])[0]
    lower_rows, upper_rows = (block(rows32, i, 0) for i in range(2))
    down_back, up_back = run(
        backward_out_kernel,
        [out((1, ROWS, WIDTH))] * 2,
        [(sums, rows_part), (above, upper_rows), (below, upper_rows), down_stash, up_stash],
    )

    rows = turned(after(run(sum_kernel, [out((RING, 2 * ROWS, PART))], [*added])[0], sums))
    down_out, up_out = run(
        forward_out_kernel,
        [out((1, ROWS, WIDTH))] * 2,
        [rows, (below, lower_rows), (above, lower_rows)],
    )
    return down_out, up_out, down_back, up_back, value_grad, output_grad


def solution(mesh):
    placed = (
        P("pipe", "tensor", None),
        P("pipe", "tensor", None),
        P("pipe", "tensor", None),
        P("pipe", "tensor", None),
        P("pipe", "tensor", None),
        P("pipe", "tensor", None),
        P(None, "tensor", None),
        P(None, "pipe", None),
        P("pipe", None, None, "tensor"),
        P("pipe", None, "tensor", None),
    )
    return jax.shard_map(
        local,
        mesh=mesh,
        in_specs=placed,
        out_specs=(
            P("pipe", "tensor", None),
            P("pipe", "tensor", None),
            P("pipe", "tensor", None),
            P("pipe", "tensor", None),
            P("pipe", None, "tensor"),
            P("pipe", "tensor", None),
        ),
        check_vma=False,
    )
```
